32 devices in a mesh: groups: 2 (over x), seq: 16 (over z, y, core).
Axes of the slice: x: 2, y: 2, z: 4, core: 2. Of those that a mesh axis runs over, the one named last changes fastest.
Arguments:
- dna_rows: bfloat16 [12, 1024, 768], P('groups', 'seq'), parts along dimension 0, may hold values from -6 to 6
- conv_weight: bfloat16 [5, 768, 768], replicated, may hold values from -0.09375 to 0.09375
- norm_gain: float32 [768], replicated, may hold values from 0.5 to 1.5
- w_query: bfloat16 [768, 768], replicated, may hold values from -3 to 3
- w_key: bfloat16 [768, 768], replicated, may hold values from -0.4375 to 0.4375
- w_value: bfloat16 [768, 768], replicated, may hold values from -0.21875 to 0.21875
- w_out: bfloat16 [768, 768], replicated, may hold values from -0.21875 to 0.21875
Outputs:
- pooled: bfloat16 [12, 512, 768], P('groups', 'seq'), parts along dimension 0
- attended: bfloat16 [12, 512, 768], P('groups', 'seq'), parts along dimension 0
The draws below stay inside these ranges and needn't reach their ends.
There are 2 independent parts, one for each index of `groups`. The reference program is written for one: setup_inputs(seed, part) draws one part's arguments, and reference() takes and returns one part's arrays. A program takes and returns all parts, laid end to end along the dimension named above; an argument that names none is the same for every part. Nothing has to cross between parts.
All inputs are finite; a program needn't handle non-finite values.
Results may differ from the reference program's by a relative error of at most 0.038.
Values may be sent and summed in bfloat16 or wider, within the bound.
A program may use at most 128 MiB of HBM per device.

```python
import math
import jax
import jax.numpy as jnp
from jax import lax

D = 768
HEADS = 8
TAPS = 5
DILATE = 2
SEQS = 6
ROWS = 1024


def draw_w_query(key, part):
    base = jax.random.normal(key, (D, D), jnp.float32)
    factor = 4.0
    return jnp.clip(base * factor / math.sqrt(D), -3.0, 3.0).astype(jnp.bfloat16)


def levels(rng, dims, cuts, low, top_value):
    def one(dim, shards_of):
        steps = jax.random.uniform(jax.random.fold_in(jax.random.fold_in(rng, 6), dim), (shards_of,), jnp.float32, low / len(cuts), top_value / len(cuts))
        return jnp.repeat(jnp.exp(steps), dims[dim] // shards_of).reshape((-1,) + (1,) * (len(dims) - dim - 1))

    factor_of = one(*cuts[0])
    for cut in cuts[1:]:
        factor_of = factor_of * one(*cut)
    return factor_of


def normal_values(stream_key, extent, deviation, bound, cuts=(), dtype=jnp.bfloat16):
    entries = deviation * jax.random.normal(stream_key, extent, jnp.float32)
    if cuts:
        entries = entries * levels(stream_key, extent, cuts, -0.22, 0.18)
    return jnp.clip(entries, -bound, bound).astype(dtype)


def setup_inputs(seed: int = 0, part: int = 0) -> dict:
    arg_keys = jax.random.split(jax.random.key(seed), 8)
    own_keys = jax.random.split(jax.random.fold_in(arg_keys[7], part), 8)
    dna_rows = normal_values(own_keys[0], (SEQS, ROWS, D), 1.0, 6.0, ((1, 16),))
    conv_weight = normal_values(arg_keys[1], (TAPS, D, D), (TAPS * D) ** -0.5, 0.09375)
    norm_gain = jnp.clip(1.0 + 0.1 * jax.random.normal(arg_keys[2], (D,), jnp.float32), 0.5, 1.5)
    w_query = draw_w_query(jax.random.fold_in(arg_keys[7], 71), part)
    w_key = normal_values(arg_keys[4], (D, D), (D // 4) ** -0.5, 0.4375)
    w_value = normal_values(arg_keys[5], (D, D), D ** -0.5, 0.21875)
    w_out = normal_values(arg_keys[6], (D, D), D ** -0.5, 0.21875)
    return dict(dna_rows=dna_rows, conv_weight=conv_weight, norm_gain=norm_gain, w_query=w_query, w_key=w_key, w_value=w_value, w_out=w_out)


def reference(dna_rows, conv_weight, norm_gain, w_query, w_key, w_value, w_out):
    seq_count, row_total, channels = dna_rows.shape
    margin_rows = 2 * DILATE
    padded_input = jnp.pad(dna_rows, ((0, 0), (margin_rows, margin_rows), (0, 0)))
    conv_sum = jnp.zeros((seq_count * row_total, channels), jnp.float32)
    for offset in range(TAPS):
        window = lax.slice_in_dim(padded_input, offset * DILATE, offset * DILATE + row_total, axis=1)
        conv_sum = conv_sum + jnp.dot(window.reshape(-1, channels), conv_weight[offset], preferred_element_type=jnp.float32)
    encoded = dna_rows.reshape(-1, channels).astype(jnp.float32) + jax.nn.gelu(conv_sum)
    pooled = encoded.reshape(seq_count, row_total // 2, 2, channels).mean(axis=2).astype(jnp.bfloat16)
    widened = pooled.astype(jnp.float32)
    normed = (widened * lax.rsqrt(lax.optimization_barrier(jnp.mean(widened * widened, axis=-1, keepdims=True)) + 1e-06) * norm_gain).astype(jnp.bfloat16)
    flattened = normed.reshape(-1, channels)
    positions = row_total // 2
    head_size = channels // HEADS

    def project(weight_matrix):
        made = jnp.dot(flattened, weight_matrix, preferred_element_type=jnp.float32).astype(jnp.bfloat16)
        return made.reshape(seq_count, positions, HEADS, head_size).transpose(0, 2, 1, 3).reshape(seq_count * HEADS, positions, head_size)
    query_heads = project(w_query)
    key_heads = project(w_key)
    value_heads = project(w_value)
    block_rows = min(512, positions)
    scale = 1.0 / math.sqrt(head_size)

    def one_head(operands):
        query_one, key_one, value_one = operands

        def one_block(query_block):
            score_matrix = jnp.dot(query_block, key_one.T, preferred_element_type=jnp.float32) * scale
            row_max = lax.optimization_barrier(jnp.max(score_matrix, axis=-1, keepdims=True))
            exp_terms = jnp.exp(score_matrix - row_max)
            row_sum = lax.optimization_barrier(jnp.sum(exp_terms, axis=-1, keepdims=True))
            mixed = jnp.dot(exp_terms.astype(jnp.bfloat16), value_one, preferred_element_type=jnp.float32)
            return (mixed / row_sum).astype(jnp.bfloat16)
        return lax.map(one_block, query_one.reshape(-1, block_rows, head_size)).reshape(positions, head_size)
    heads_out = lax.map(one_head, (query_heads, key_heads, value_heads))
    joined = heads_out.reshape(seq_count, HEADS, positions, head_size).transpose(0, 2, 1, 3).reshape(-1, channels)
    attended = jnp.dot(joined, w_out, preferred_element_type=jnp.float32).astype(jnp.bfloat16)
    return (pooled, attended.reshape(seq_count, positions, channels))
```

```python
import functools
import math

import jax
import jax.numpy as jnp
from jax import lax
from jax.experimental import pallas as pl
from jax.experimental.pallas import tpu as pltpu
from jax.sharding import PartitionSpec as P

HEADS = 8
TAPS = 5
DILATE = 2
LANES = 128
COLUMN_TILE = 256
MESH = pl.DeviceIdType.MESH


def kernel(
    n, seqs, rows,
    x_ref, conv_hbm, gain_ref, wq_hbm, wk_hbm, wv_hbm, wo_hbm,
    pooled_ref, attended_ref,
    conv_w, wq, wk, wv, wo,
    pad, taps, edge_out, edge_in, packed, got, mixed, back,
    conv_sem, w_sem, edge_send, edge_recv, pack_send, pack_recv, pack_local,
    back_send, back_recv, back_local,
):
    channels = x_ref.shape[-1]
    head = channels // HEADS
    half = rows // 2
    group = 2 * HEADS
    units = seqs // 2
    reach = 2 * DILATE
    pitch = rows + 2 * reach
    me = lax.axis_index("seq")
    mine = lax.rem(me, group)
    block = me - mine

    tiles = channels // COLUMN_TILE
    conv_copies = []
    for j in range(tiles):
        cols = pl.ds(j * COLUMN_TILE, COLUMN_TILE)
        conv_copies.append(
            pltpu.make_async_copy(conv_hbm.at[:, cols], conv_w.at[:, cols], conv_sem.at[j])
        )
    w_copies = [
        pltpu.make_async_copy(a, b, w_sem.at[i])
        for i, (a, b) in enumerate(((wq_hbm, wq), (wk_hbm, wk), (wv_hbm, wv), (wo_hbm, wo)))
    ]
    barrier = pltpu.get_barrier_semaphore()

    def greet(k, carry):
        pl.semaphore_signal(
            barrier, inc=1, device_id={"seq": lax.rem(me + k, n)}, device_id_type=MESH
        )
        return carry

    lax.fori_loop(1, n, greet, 0)
    for copy in conv_copies + w_copies:
        copy.start()

    for b in range(seqs):
        edge_out[0, b * reach : (b + 1) * reach, :] = x_ref[b, :8, :].astype(jnp.float32)[:reach]
        edge_out[1, b * reach : (b + 1) * reach, :] = x_ref[b, rows - 8 :, :].astype(jnp.float32)[
            8 - reach :
        ]
    pl.semaphore_wait(barrier, n - 1)

    def edge(side, target):
        return pltpu.make_async_remote_copy(
            src_ref=edge_out.at[side],
            dst_ref=edge_in.at[side],
            send_sem=edge_send.at[side],
            recv_sem=edge_recv.at[side],
            device_id={"seq": target},
            device_id_type=MESH,
        )

    to_left = edge(0, lax.rem(me + n - 1, n))
    to_right = edge(1, lax.rem(me + 1, n))
    to_left.start()
    to_right.start()
    strips = channels // LANES
    for b in range(seqs):
        for j in range(strips):
            strip = slice(j * LANES, (j + 1) * LANES)
            pad[j, b * pitch + reach : b * pitch + reach + rows, :] = x_ref[b, :, strip].astype(
                jnp.float32
            )
    to_left.wait()
    to_right.wait()
    has_left = jnp.where(me > 0, 1.0, 0.0).astype(jnp.float32)
    has_right = jnp.where(me < n - 1, 1.0, 0.0).astype(jnp.float32)
    for b in range(seqs):
        for j in range(strips):
            strip = slice(j * LANES, (j + 1) * LANES)
            pad[j, b * pitch : b * pitch + reach, :] = (
                edge_in[1, b * reach : (b + 1) * reach, strip] * has_left
            )
            pad[j, b * pitch + reach + rows : (b + 1) * pitch, :] = (
                edge_in[0, b * reach : (b + 1) * reach, strip] * has_right
            )

    for t in range(TAPS):
        for parity in range(2):
            for b in range(seqs):
                start = b * pitch + t * DILATE + parity
                to = (parity * seqs + b) * half
                for j in range(strips):
                    at = t * channels + j * LANES
                    taps[to : to + half, at : at + LANES] = (
                        pad[j, pl.ds(start, half, stride=2), :]
                    ).astype(jnp.bfloat16)

    count = seqs * half
    squares = jnp.zeros((count, 1), jnp.float32)
    middle = (TAPS // 2) * channels
    for j in range(tiles):
        conv_copies[j].wait()
        cols = slice(j * COLUMN_TILE, (j + 1) * COLUMN_TILE)
        conv_sum = jnp.dot(taps[...], conv_w[:, cols], preferred_element_type=jnp.float32)
        here = taps[:, middle + j * COLUMN_TILE : middle + (j + 1) * COLUMN_TILE]
        encoded = here.astype(jnp.float32) + jax.nn.gelu(conv_sum)
        pooled = ((encoded[:count] + encoded[count:]) * 0.5).astype(jnp.bfloat16)
        pooled_ref[:, cols] = pooled
        wide = pooled.astype(jnp.float32)
        squares = squares + jnp.sum(wide * wide, axis=-1, keepdims=True)
    shrink = lax.rsqrt(squares * (1.0 / channels) + 1e-06)
    normed = (pooled_ref[...].astype(jnp.float32) * shrink * gain_ref[...]).astype(jnp.bfloat16)

    projected = []
    for i, w in enumerate((wq, wk, wv)):
        w_copies[i].wait()
        projected.append(jnp.dot(normed, w[...], preferred_element_type=jnp.float32))

    width = packed.shape[-1]
    fill = jnp.zeros((half, width - 3 * units * head), jnp.float32)
    for g in range(group):
        h = g % HEADS
        pieces = []
        for c in range(units):
            b = 2 * c + g // HEADS
            for made in projected:
                pieces.append(made[b * half : (b + 1) * half, h * head : (h + 1) * head])
        packed[g] = jnp.concatenate(pieces + [fill], axis=-1).astype(jnp.bfloat16)

    bounds = [0] + [-(-3 * head * (c + 1) // LANES) * LANES for c in range(units)]
    parts = [pl.ds(bounds[c], bounds[c + 1] - bounds[c]) for c in range(units)]
    for c in range(units):
        pltpu.make_async_copy(
            packed.at[mine, :, parts[c]], got.at[me, :, parts[c]], pack_local.at[c]
        ).start()

        def scatter(k, carry, c=c):
            target = lax.rem(me + k, n)
            pltpu.make_async_remote_copy(
                src_ref=packed.at[lax.rem(target, group), :, parts[c]],
                dst_ref=got.at[me, :, parts[c]],
                send_sem=pack_send.at[c],
                recv_sem=pack_recv.at[c],
                device_id={"seq": target},
                device_id_type=MESH,
            ).start()
            return carry

        lax.fori_loop(1, n, scatter, 0)

    total = n * half
    queries = group * half
    step = 4 * half
    factor = math.log2(math.e) / math.sqrt(head)
    for c in range(units):
        pltpu.make_async_copy(
            packed.at[mine, :, parts[c]], got.at[me, :, parts[c]], pack_local.at[c]
        ).wait()
        others = got.at[pl.ds(0, n - 1), :, parts[c]]
        pltpu.make_async_copy(others, others, pack_recv.at[c]).wait()
        base = 3 * c * head
        keys = got[:, :, base + head : base + 2 * head].reshape(total, head)
        values = got[:, :, base + 2 * head : base + 3 * head].reshape(total, head)
        for q in range(queries // step):
            sources = step // half
            query = got[pl.ds(block + q * sources, sources), :, base : base + head].reshape(
                step, head
            )
            scores = lax.dot_general(
                query, keys, (((1,), (1,)), ((), ())), preferred_element_type=jnp.float32
            )
            top = jnp.max(scores, axis=-1, keepdims=True)
            terms = jnp.exp2((scores - top) * factor)
            row_sum = jnp.sum(terms, axis=-1, keepdims=True)
            out = jnp.dot(terms.astype(jnp.bfloat16), values, preferred_element_type=jnp.float32)
            out = (out / row_sum).astype(jnp.bfloat16)
            mixed[c, q * sources : (q + 1) * sources, :, :head] = out.reshape(sources, half, head)
        pltpu.make_async_copy(
            mixed.at[c, mine], back.at[c, mine], back_local.at[c]
        ).start()
        for k in range(1, group):
            index = lax.rem(mine + k, group)
            pltpu.make_async_remote_copy(
                src_ref=mixed.at[c, index],
                dst_ref=back.at[c, mine],
                send_sem=back_send.at[c],
                recv_sem=back_recv.at[c],
                device_id={"seq": block + index},
                device_id_type=MESH,
            ).start()

    w_copies[3].wait()
    for c in range(units):
        pltpu.make_async_copy(mixed.at[c, mine], back.at[c, mine], back_local.at[c]).wait()
        others = back.at[c, pl.ds(0, group - 1)]
        pltpu.make_async_copy(others, others, back_recv.at[c]).wait()
        attended = jnp.zeros((2 * half, channels), jnp.float32)
        for h in range(HEADS):
            both = jnp.concatenate(
                [back[c, h, :, :head], back[c, HEADS + h, :, :head]], axis=0
            )
            attended = attended + jnp.dot(
                both, wo[h * head : (h + 1) * head, :], preferred_element_type=jnp.float32
            )
        attended_ref[c * 2 * half : (c + 1) * 2 * half, :] = attended.astype(jnp.bfloat16)

    for c in range(units):
        others = got.at[pl.ds(0, n - 1), :, parts[c]]
        pltpu.make_async_copy(others, others, pack_send.at[c]).wait()
        others = back.at[c, pl.ds(0, group - 1)]
        pltpu.make_async_copy(others, others, back_send.at[c]).wait()


def on_device(dna_rows, conv_weight, norm_gain, w_query, w_key, w_value, w_out):
    n = lax.axis_size("seq")
    seqs, rows, channels = dna_rows.shape
    half = rows // 2
    group = 2 * HEADS
    units = seqs // 2
    head = channels // HEADS
    width = -(-3 * units * head // LANES) * LANES
    reach = 2 * DILATE
    bf16, f32 = jnp.bfloat16, jnp.float32
    vmem = pl.BlockSpec(memory_space=pltpu.VMEM)
    far = pl.BlockSpec(memory_space=pl.ANY)
    square = pltpu.VMEM((channels, channels), bf16)
    dma = pltpu.SemaphoreType.DMA
    pooled, attended = pl.pallas_call(
        functools.partial(kernel, n, seqs, rows),
        out_shape=[jax.ShapeDtypeStruct((seqs * half, channels), bf16)] * 2,
        in_specs=[vmem, far, vmem, far, far, far, far],
        out_specs=[vmem, vmem],
        scratch_shapes=[
            pltpu.VMEM((TAPS * channels, channels), bf16),
            square, square, square, square,
            pltpu.VMEM((channels // LANES, seqs * (rows + 2 * reach), LANES), f32),
            pltpu.VMEM((seqs * rows, TAPS * channels), bf16),
            pltpu.VMEM((2, seqs * reach, channels), f32),
            pltpu.VMEM((2, seqs * reach, channels), f32),
            pltpu.VMEM((group, half, width), bf16),
            pltpu.VMEM((n, half, width), bf16),
            pltpu.VMEM((units, group, half, LANES), bf16),
            pltpu.VMEM((units, group, half, LANES), bf16),
            dma((channels // COLUMN_TILE,)), dma((4,)),
            dma((2,)), dma((2,)),
            dma((units,)), dma((units,)), dma((units,)),
            dma((units,)), dma((units,)), dma((units,)),
        ],
        compiler_params=pltpu.CompilerParams(
            collective_id=0, has_side_effects=True, vmem_limit_bytes=56 * 1024 * 1024
        ),
    )(
        dna_rows,
        conv_weight.reshape(TAPS * channels, channels),
        norm_gain.reshape(1, channels),
        w_query, w_key, w_value, w_out,
    )
    return pooled.reshape(seqs, half, channels), attended.reshape(seqs, half, channels)


def solution(mesh):
    placed = (P("groups", "seq", None), P(), P(), P(), P(), P(), P())
    return jax.shard_map(
        on_device,
        mesh=mesh,
        in_specs=placed,
        out_specs=(P("groups", "seq", None), P("groups", "seq", None)),
        check_vma=False,
    )
```

```python
import functools
import math

import jax
import jax.numpy as jnp
from jax import lax
from jax.experimental import pallas as pl
from jax.experimental.pallas import tpu as pltpu
from jax.sharding import PartitionSpec as P

HEADS = 8
TAPS = 5
DILATE = 2
LANES = 128
COLUMN_TILE = 256
GROUP = 16
QUERY_ROWS = 256
MESH = pl.DeviceIdType.MESH


def kernel(
    n, seqs, rows,
    x_ref, conv_hbm, gain_ref, wq_hbm, wk_hbm, wv_hbm, wo_hbm,
    pooled_ref, attended_ref,
    conv_w, wq, wk, wv, wo,
    pad, taps, edge_out, edge_in, outgoing, got, q_rows, k_rows, v_rows, mixed, back,
    conv_sem, w_sem, edge_send, edge_recv, pack_sems, back_sems,
):
    channels = x_ref.shape[-1]
    head = channels // HEADS
    part = channels // 2
    half = rows // 2
    reach = 2 * DILATE
    slots = 2 * seqs
    idle = (GROUP - slots) // 2
    pitch = rows + 2 * reach
    me = lax.axis_index("seq")
    mine = lax.rem(me, GROUP)
    block = me - mine
    slot = mine - idle
    active = jnp.logical_and(slot >= 0, slot < slots)

    tiles = channels // COLUMN_TILE
    conv_copies = []
    for j in range(tiles):
        cols = pl.ds(j * COLUMN_TILE, COLUMN_TILE)
        conv_copies.append(
            pltpu.make_async_copy(conv_hbm.at[:, cols], conv_w.at[:, cols], conv_sem.at[j])
        )
    w_copies = [
        pltpu.make_async_copy(a, b, w_sem.at[i])
        for i, (a, b) in enumerate(((wq_hbm, wq), (wk_hbm, wk), (wv_hbm, wv), (wo_hbm, wo)))
    ]
    barrier = pltpu.get_barrier_semaphore()

    def greet(k, carry):
        pl.semaphore_signal(
            barrier, inc=1, device_id={"seq": lax.rem(me + k, n)}, device_id_type=MESH
        )
        return carry

    lax.fori_loop(1, n, greet, 0)
    for copy in conv_copies + w_copies:
        copy.start()

    for b in range(seqs):
        edge_out[0, b * reach : (b + 1) * reach, :] = x_ref[b, :8, :].astype(jnp.float32)[:reach]
        edge_out[1, b * reach : (b + 1) * reach, :] = x_ref[b, rows - 8 :, :].astype(jnp.float32)[
            8 - reach :
        ]
    pl.semaphore_wait(barrier, n - 1)

    def edge(side, target):
        return pltpu.make_async_remote_copy(
            src_ref=edge_out.at[side],
            dst_ref=edge_in.at[side],
            send_sem=edge_send.at[side],
            recv_sem=edge_recv.at[side],
            device_id={"seq": target},
            device_id_type=MESH,
        )

    to_left = edge(0, lax.rem(me + n - 1, n))
    to_right = edge(1, lax.rem(me + 1, n))
    to_left.start()
    to_right.start()
    strips = channels // LANES
    for b in range(seqs):
        for j in range(strips):
            strip = slice(j * LANES, (j + 1) * LANES)
            pad[j, b * pitch + reach : b * pitch + reach + rows, :] = x_ref[b, :, strip].astype(
                jnp.float32
            )
    to_left.wait()
    to_right.wait()
    has_left = jnp.where(me > 0, 1.0, 0.0).astype(jnp.float32)
    has_right = jnp.where(me < n - 1, 1.0, 0.0).astype(jnp.float32)
    for b in range(seqs):
        for j in range(strips):
            strip = slice(j * LANES, (j + 1) * LANES)
            pad[j, b * pitch : b * pitch + reach, :] = (
                edge_in[1, b * reach : (b + 1) * reach, strip] * has_left
            )
            pad[j, b * pitch + reach + rows : (b + 1) * pitch, :] = (
                edge_in[0, b * reach : (b + 1) * reach, strip] * has_right
            )

    for t in range(TAPS):
        for parity in range(2):
            for b in range(seqs):
                start = b * pitch + t * DILATE + parity
                to = (parity * seqs + b) * half
                for j in range(strips):
                    at = t * channels + j * LANES
                    taps[to : to + half, at : at + LANES] = (
                        pad[j, pl.ds(start, half, stride=2), :]
                    ).astype(jnp.bfloat16)

    count = seqs * half
    squares = jnp.zeros((count, 1), jnp.float32)
    middle = (TAPS // 2) * channels
    for j in range(tiles):
        conv_copies[j].wait()
        cols = slice(j * COLUMN_TILE, (j + 1) * COLUMN_TILE)
        conv_sum = jnp.dot(taps[...], conv_w[:, cols], preferred_element_type=jnp.float32)
        here = taps[:, middle + j * COLUMN_TILE : middle + (j + 1) * COLUMN_TILE]
        encoded = here.astype(jnp.float32) + jax.nn.gelu(conv_sum)
        pooled = ((encoded[:count] + encoded[count:]) * 0.5).astype(jnp.bfloat16)
        pooled_ref[:, cols] = pooled
        wide = pooled.astype(jnp.float32)
        squares = squares + jnp.sum(wide * wide, axis=-1, keepdims=True)
    shrink = lax.rsqrt(squares * (1.0 / channels) + 1e-06)
    normed = (pooled_ref[...].astype(jnp.float32) * shrink * gain_ref[...]).astype(jnp.bfloat16)

    for b in range(seqs):
        outgoing[b] = normed[b * half : (b + 1) * half]

    sends = slots * (n // GROUP)
    pack_send, pack_recv, pack_local = (pack_sems.at[i] for i in range(3))
    back_send, back_recv, back_local = (back_sems.at[i] for i in range(3))
    window = jnp.clip(slot, 0, slots - 1) // 2
    lanes = pl.ds(pl.multiple_of(lax.rem(jnp.clip(slot, 0, slots - 1), 2) * part, LANES), part)
    own = pltpu.make_async_copy(outgoing.at[window], got.at[me], pack_local)

    @pl.when(active)
    def _():
        own.start()

    def scatter(k, carry):
        to = lax.rem(k + mine, slots)
        target = (k // slots) * GROUP + idle + to

        @pl.when(target != me)
        def _():
            pltpu.make_async_remote_copy(
                src_ref=outgoing.at[to // 2],
                dst_ref=got.at[me],
                send_sem=pack_send,
                recv_sem=pack_recv,
                device_id={"seq": target},
                device_id_type=MESH,
            ).start()

        return carry

    lax.fori_loop(0, sends, scatter, 0)
    for copy in w_copies:
        copy.wait()

    def settle(ref, count, sem):
        some = ref.at[pl.ds(0, count)]
        pltpu.make_async_copy(some, some, sem).wait()

    kept = pltpu.make_async_copy(mixed.at[mine], back.at[jnp.clip(slot, 0, slots - 1)], back_local)
    factor = math.log2(math.e) / math.sqrt(head)

    @pl.when(active)
    def _():
        own.wait()
        settle(got, n - 1, pack_recv)

        def project(i, carry):
            made = got[pl.ds(i * GROUP, GROUP)].reshape(GROUP * half, channels)
            at = pl.ds(pl.multiple_of(i * (GROUP * half), GROUP * half), GROUP * half)
            k_rows[at, :] = jnp.dot(
                made, wk[:, lanes], preferred_element_type=jnp.float32
            ).astype(jnp.bfloat16)
            v_rows[at, :] = jnp.dot(
                made, wv[:, lanes], preferred_element_type=jnp.float32
            ).astype(jnp.bfloat16)
            return carry

        lax.fori_loop(0, n // GROUP, project, 0)
        asking = got[pl.ds(block, GROUP)].reshape(GROUP * half, channels)
        q_rows[...] = jnp.dot(
            asking, wq[:, lanes], preferred_element_type=jnp.float32
        ).astype(jnp.bfloat16)
        sources = QUERY_ROWS // half
        for q in range(GROUP // sources):
            outs = []
            for h in range(HEADS // 2):
                of_head = slice(h * head, (h + 1) * head)
                scores = lax.dot_general(
                    q_rows[q * QUERY_ROWS : (q + 1) * QUERY_ROWS, of_head],
                    k_rows[:, of_head],
                    (((1,), (1,)), ((), ())),
                    preferred_element_type=jnp.float32,
                )
                top = jnp.max(scores, axis=-1, keepdims=True)
                terms = jnp.exp2((scores - top) * factor)
                row_sum = jnp.sum(terms, axis=-1, keepdims=True)
                out = jnp.dot(
                    terms.astype(jnp.bfloat16),
                    v_rows[:, of_head],
                    preferred_element_type=jnp.float32,
                )
                outs.append(out / row_sum)
            joined = jnp.concatenate(outs, axis=-1).astype(jnp.bfloat16)
            mixed[q * sources : (q + 1) * sources] = joined.reshape(sources, half, part)
            for k in range(q * sources, (q + 1) * sources):

                @pl.when(mine != k)
                def _(k=k):
                    pltpu.make_async_remote_copy(
                        src_ref=mixed.at[k],
                        dst_ref=back.at[slot],
                        send_sem=back_send,
                        recv_sem=back_recv,
                        device_id={"seq": block + k},
                        device_id_type=MESH,
                    ).start()

                @pl.when(mine == k)
                def _():
                    kept.start()

        kept.wait()
        settle(back, slots - 1, back_recv)
        settle(mixed, GROUP - 1, back_send)
        settle(got, sends - 1, pack_send)

    @pl.when(jnp.logical_not(active))
    def _():
        settle(back, slots, back_recv)
        settle(got, sends, pack_send)

    attended = jnp.zeros((count, channels), jnp.float32)
    for i in range(2):
        joined = jnp.concatenate([back[2 * b + i] for b in range(seqs)], axis=0)
        attended = attended + jnp.dot(
            joined, wo[i * part : (i + 1) * part, :], preferred_element_type=jnp.float32
        )
    attended_ref[...] = attended.astype(jnp.bfloat16)


def on_device(dna_rows, conv_weight, norm_gain, w_query, w_key, w_value, w_out):
    n = lax.axis_size("seq")
    seqs, rows, channels = dna_rows.shape
    half = rows // 2
    part = channels // 2
    reach = 2 * DILATE
    bf16, f32 = jnp.bfloat16, jnp.float32
    vmem = pl.BlockSpec(memory_space=pltpu.VMEM)
    far = pl.BlockSpec(memory_space=pl.ANY)
    square = pltpu.VMEM((channels, channels), bf16)
    dma = pltpu.SemaphoreType.DMA
    pooled, attended = pl.pallas_call(
        functools.partial(kernel, n, seqs, rows),
        out_shape=[jax.ShapeDtypeStruct((seqs * half, channels), bf16)] * 2,
        in_specs=[vmem, far, vmem, far, far, far, far],
        out_specs=[vmem, vmem],
        scratch_shapes=[
            pltpu.VMEM((TAPS * channels, channels), bf16),
            square, square, square, square,
            pltpu.VMEM((channels // LANES, seqs * (rows + 2 * reach), LANES), f32),
            pltpu.VMEM((seqs * rows, TAPS * channels), bf16),
            pltpu.VMEM((2, seqs * reach, channels), f32),
            pltpu.VMEM((2, seqs * reach, channels), f32),
            pltpu.VMEM((seqs, half, channels), bf16),
            pltpu.VMEM((n, half, channels), bf16),
            pltpu.VMEM((GROUP * half, part), bf16),
            pltpu.VMEM((n * half, part), bf16),
            pltpu.VMEM((n * half, part), bf16),
            pltpu.VMEM((GROUP, half, part), bf16),
            pltpu.VMEM((2 * seqs, half, part), bf16),
            dma((channels // COLUMN_TILE,)), dma((4,)),
            dma((2,)), dma((2,)),
            dma((3,)), dma((3,)),
        ],
        compiler_params=pltpu.CompilerParams(
            collective_id=0, has_side_effects=True, vmem_limit_bytes=56 * 1024 * 1024
        ),
    )(
        dna_rows,
        conv_weight.reshape(TAPS * channels, channels),
        norm_gain.reshape(1, channels),
        w_query, w_key, w_value, w_out,
    )
    return pooled.reshape(seqs, half, channels), attended.reshape(seqs, half, channels)


def solution(mesh):
    placed = (P("groups", "seq", None), P(), P(), P(), P(), P(), P())
    return jax.shard_map(
        on_device,
        mesh=mesh,
        in_specs=placed,
        out_specs=(P("groups", "seq", None), P("groups", "seq", None)),
        check_vma=False,
    )
```

```python
import functools
import math

import jax
import jax.numpy as jnp
from jax import lax
from jax.experimental import pallas as pl
from jax.experimental.pallas import tpu as pltpu
from jax.sharding import PartitionSpec as P

HEADS = 8
TAPS = 5
DILATE = 2
LANES = 128
COLUMN_TILE = 256
GROUP = 16
QUERY_ROWS = 256
MESH = pl.DeviceIdType.MESH


def kernel(
    n, seqs, rows,
    x_ref, conv_hbm, gain_ref, wq_hbm, wk_hbm, wv_hbm, wo_hbm,
    pooled_ref, attended_ref,
    conv_w, wq, wk, wv, wo,
    pad, taps, edge_out, edge_in, outgoing, got, q_rows, k_rows, v_rows, mixed, back,
    conv_sem, w_sem, edge_send, edge_recv, pack_sems, back_sems, twin_sems,
):
    channels = x_ref.shape[-1]
    head = channels // HEADS
    part = channels // 2
    half = rows // 2
    reach = 2 * DILATE
    slots = 2 * seqs
    idle = (GROUP - slots) // 2
    pitch = rows + 2 * reach
    me = lax.axis_index("seq")
    mine = lax.rem(me, GROUP)
    block = me - mine
    slot = mine - idle
    active = jnp.logical_and(slot >= 0, slot < slots)

    tiles = channels // COLUMN_TILE
    conv_copies = []
    for j in range(tiles):
        cols = pl.ds(j * COLUMN_TILE, COLUMN_TILE)
        conv_copies.append(
            pltpu.make_async_copy(conv_hbm.at[:, cols], conv_w.at[:, cols], conv_sem.at[j])
        )
    w_copies = [
        pltpu.make_async_copy(a, b, w_sem.at[i])
        for i, (a, b) in enumerate(((wq_hbm, wq), (wk_hbm, wk), (wv_hbm, wv), (wo_hbm, wo)))
    ]
    barrier = pltpu.get_barrier_semaphore()

    def greet(k, carry):
        pl.semaphore_signal(
            barrier, inc=1, device_id={"seq": lax.rem(me + k, n)}, device_id_type=MESH
        )
        return carry

    lax.fori_loop(1, n, greet, 0)
    for copy in conv_copies + w_copies:
        copy.start()

    for b in range(seqs):
        edge_out[0, b * reach : (b + 1) * reach, :] = x_ref[b, :8, :].astype(jnp.float32)[:reach]
        edge_out[1, b * reach : (b + 1) * reach, :] = x_ref[b, rows - 8 :, :].astype(jnp.float32)[
            8 - reach :
        ]
    pl.semaphore_wait(barrier, n - 1)

    def edge(side, target):
        return pltpu.make_async_remote_copy(
            src_ref=edge_out.at[side],
            dst_ref=edge_in.at[side],
            send_sem=edge_send.at[side],
            recv_sem=edge_recv.at[side],
            device_id={"seq": target},
            device_id_type=MESH,
        )

    to_left = edge(0, lax.rem(me + n - 1, n))
    to_right = edge(1, lax.rem(me + 1, n))
    to_left.start()
    to_right.start()
    strips = channels // LANES
    for b in range(seqs):
        for j in range(strips):
            strip = slice(j * LANES, (j + 1) * LANES)
            pad[j, b * pitch + reach : b * pitch + reach + rows, :] = x_ref[b, :, strip].astype(
                jnp.float32
            )
    to_left.wait()
    to_right.wait()
    has_left = jnp.where(me > 0, 1.0, 0.0).astype(jnp.float32)
    has_right = jnp.where(me < n - 1, 1.0, 0.0).astype(jnp.float32)
    for b in range(seqs):
        for j in range(strips):
            strip = slice(j * LANES, (j + 1) * LANES)
            pad[j, b * pitch : b * pitch + reach, :] = (
                edge_in[1, b * reach : (b + 1) * reach, strip] * has_left
            )
            pad[j, b * pitch + reach + rows : (b + 1) * pitch, :] = (
                edge_in[0, b * reach : (b + 1) * reach, strip] * has_right
            )

    for t in range(TAPS):
        for parity in range(2):
            for b in range(seqs):
                start = b * pitch + t * DILATE + parity
                to = (parity * seqs + b) * half
                for j in range(strips):
                    at = t * channels + j * LANES
                    taps[to : to + half, at : at + LANES] = (
                        pad[j, pl.ds(start, half, stride=2), :]
                    ).astype(jnp.bfloat16)

    count = seqs * half
    squares = jnp.zeros((count, 1), jnp.float32)
    middle = (TAPS // 2) * channels
    for j in range(tiles):
        conv_copies[j].wait()
        cols = slice(j * COLUMN_TILE, (j + 1) * COLUMN_TILE)
        conv_sum = jnp.dot(taps[...], conv_w[:, cols], preferred_element_type=jnp.float32)
        here = taps[:, middle + j * COLUMN_TILE : middle + (j + 1) * COLUMN_TILE]
        encoded = here.astype(jnp.float32) + jax.nn.gelu(conv_sum)
        pooled = ((encoded[:count] + encoded[count:]) * 0.5).astype(jnp.bfloat16)
        pooled_ref[:, cols] = pooled
        wide = pooled.astype(jnp.float32)
        squares = squares + jnp.sum(wide * wide, axis=-1, keepdims=True)
    shrink = lax.rsqrt(squares * (1.0 / channels) + 1e-06)
    normed = (pooled_ref[...].astype(jnp.float32) * shrink * gain_ref[...].reshape(1, channels)).astype(jnp.bfloat16)

    for b in range(seqs):
        outgoing[b] = normed[b * half : (b + 1) * half]

    sends = seqs * (n // GROUP)
    core = lax.rem(me, 2)
    twin = me + 1 - 2 * core
    pack_send, pack_recv, pack_local = (pack_sems.at[i] for i in range(3))
    back_send, back_recv, back_local = (back_sems.at[i] for i in range(3))
    window = jnp.clip(slot, 0, slots - 1) // 2
    lanes = pl.ds(pl.multiple_of(lax.rem(jnp.clip(slot, 0, slots - 1), 2) * part, LANES), part)
    own = pltpu.make_async_copy(outgoing.at[window], got.at[me], pack_local)

    @pl.when(active)
    def _():
        own.start()

    def scatter(k, carry):
        to = lax.rem(k + mine // 2, seqs)
        target = (k // seqs) * GROUP + idle + 2 * to + core

        @pl.when(target != me)
        def _():
            pltpu.make_async_remote_copy(
                src_ref=outgoing.at[to],
                dst_ref=got.at[me],
                send_sem=pack_send,
                recv_sem=pack_recv,
                device_id={"seq": target},
                device_id_type=MESH,
            ).start()

        return carry

    lax.fori_loop(0, sends, scatter, 0)
    for copy in w_copies:
        copy.wait()

    def settle(ref, count, sem):
        some = ref.at[pl.ds(0, count)]
        pltpu.make_async_copy(some, some, sem).wait()

    kept = pltpu.make_async_copy(mixed.at[mine], back.at[jnp.clip(slot, 0, slots - 1)], back_local)
    factor = math.log2(math.e) / math.sqrt(head)

    @pl.when(active)
    def _():
        own.wait()
        settle(got, n // 2 - 1, pack_recv)

        def relay(i, carry):
            pltpu.make_async_remote_copy(
                src_ref=got.at[2 * i + core],
                dst_ref=got.at[2 * i + core],
                send_sem=twin_sems.at[0],
                recv_sem=twin_sems.at[1],
                device_id={"seq": twin},
                device_id_type=MESH,
            ).start()
            return carry

        lax.fori_loop(0, n // 2, relay, 0)
        settle(got, n // 2, twin_sems.at[1])

        def project(i, carry):
            made = got[pl.ds(i * GROUP, GROUP)].reshape(GROUP * half, channels)
            at = pl.ds(pl.multiple_of(i * (GROUP * half), GROUP * half), GROUP * half)
            k_rows[at, :] = jnp.dot(
                made, wk[:, lanes], preferred_element_type=jnp.float32
            ).astype(jnp.bfloat16)
            v_rows[at, :] = jnp.dot(
                made, wv[:, lanes], preferred_element_type=jnp.float32
            ).astype(jnp.bfloat16)
            return carry

        lax.fori_loop(0, n // GROUP, project, 0)
        asking = got[pl.ds(block, GROUP)].reshape(GROUP * half, channels)
        q_rows[...] = jnp.dot(
            asking, wq[:, lanes], preferred_element_type=jnp.float32
        ).astype(jnp.bfloat16)
        sources = QUERY_ROWS // half
        for q in range(GROUP // sources):
            outs = []
            for h in range(HEADS // 2):
                of_head = slice(h * head, (h + 1) * head)
                scores = lax.dot_general(
                    q_rows[q * QUERY_ROWS : (q + 1) * QUERY_ROWS, of_head],
                    k_rows[:, of_head],
                    (((1,), (1,)), ((), ())),
                    preferred_element_type=jnp.float32,
                )
                top = jnp.max(scores, axis=-1, keepdims=True)
                terms = jnp.exp2((scores - top) * factor)
                row_sum = jnp.sum(terms, axis=-1, keepdims=True)
                out = jnp.dot(
                    terms.astype(jnp.bfloat16),
                    v_rows[:, of_head],
                    preferred_element_type=jnp.float32,
                )
                outs.append(out / row_sum)
            joined = jnp.concatenate(outs, axis=-1).astype(jnp.bfloat16)
            mixed[q * sources : (q + 1) * sources] = joined.reshape(sources, half, part)
            for k in range(q * sources, (q + 1) * sources):

                @pl.when(mine != k)
                def _(k=k):
                    pltpu.make_async_remote_copy(
                        src_ref=mixed.at[k],
                        dst_ref=back.at[slot],
                        send_sem=back_send,
                        recv_sem=back_recv,
                        device_id={"seq": block + k},
                        device_id_type=MESH,
                    ).start()

                @pl.when(mine == k)
                def _():
                    kept.start()

        kept.wait()
        settle(back, slots - 1, back_recv)
        settle(mixed, GROUP - 1, back_send)
        settle(got, n // 2, twin_sems.at[0])
        settle(got, sends - 1, pack_send)

    @pl.when(jnp.logical_not(active))
    def _():
        settle(back, slots, back_recv)
        settle(got, sends, pack_send)

    attended = jnp.zeros((count, channels), jnp.float32)
    for i in range(2):
        joined = jnp.concatenate([back[2 * b + i] for b in range(seqs)], axis=0)
        attended = attended + jnp.dot(
            joined, wo[i * part : (i + 1) * part, :], preferred_element_type=jnp.float32
        )
    attended_ref[...] = attended.astype(jnp.bfloat16)


def on_device(dna_rows, conv_weight, norm_gain, w_query, w_key, w_value, w_out):
    n = lax.axis_size("seq")
    seqs, rows, channels = dna_rows.shape
    half = rows // 2
    part = channels // 2
    reach = 2 * DILATE
    bf16, f32 = jnp.bfloat16, jnp.float32
    vmem = pl.BlockSpec(memory_space=pltpu.VMEM)
    far = pl.BlockSpec(memory_space=pl.ANY)
    square = pltpu.VMEM((channels, channels), bf16)
    dma = pltpu.SemaphoreType.DMA
    pooled, attended = pl.pallas_call(
        functools.partial(kernel, n, seqs, rows),
        out_shape=[jax.ShapeDtypeStruct((seqs * half, channels), bf16)] * 2,
        in_specs=[vmem, far, vmem, far, far, far, far],
        out_specs=[vmem, vmem],
        scratch_shapes=[
            pltpu.VMEM((TAPS * channels, channels), bf16),
            square, square, square, square,
            pltpu.VMEM((channels // LANES, seqs * (rows + 2 * reach), LANES), f32),
            pltpu.VMEM((seqs * rows, TAPS * channels), bf16),
            pltpu.VMEM((2, seqs * reach, channels), f32),
            pltpu.VMEM((2, seqs * reach, channels), f32),
            pltpu.VMEM((seqs, half, channels), bf16),
            pltpu.VMEM((n, half, channels), bf16),
            pltpu.VMEM((GROUP * half, part), bf16),
            pltpu.VMEM((n * half, part), bf16),
            pltpu.VMEM((n * half, part), bf16),
            pltpu.VMEM((GROUP, half, part), bf16),
            pltpu.VMEM((2 * seqs, half, part), bf16),
            dma((channels // COLUMN_TILE,)), dma((4,)),
            dma((2,)), dma((2,)),
            dma((3,)), dma((3,)), dma((2,)),
        ],
        compiler_params=pltpu.CompilerParams(
            collective_id=0, has_side_effects=True, vmem_limit_bytes=56 * 1024 * 1024
        ),
    )(
        dna_rows,
        conv_weight.reshape(TAPS * channels, channels),
        norm_gain,
        w_query, w_key, w_value, w_out,
    )
    return pooled.reshape(seqs, half, channels), attended.reshape(seqs, half, channels)


def solution(mesh):
    placed = (P("groups", "seq", None), P(), P(), P(), P(), P(), P())
    return jax.shard_map(
        on_device,
        mesh=mesh,
        in_specs=placed,
        out_specs=(P("groups", "seq", None), P("groups", "seq", None)),
        check_vma=False,
    )
```

```python
import functools
import math

import jax
import jax.numpy as jnp
from jax import lax
from jax.experimental import pallas as pl
from jax.experimental.pallas import tpu as pltpu
from jax.sharding import PartitionSpec as P

HEADS = 8
TAPS = 5
DILATE = 2
LANES = 128
COLUMN_TILE = 256
GROUP = 16
STAGES = 3
QUERY_ROWS = 256
MESH = pl.DeviceIdType.MESH


def kernel(
    n, seqs, rows,
    x_ref, conv_hbm, gain_ref, wq_hbm, wk_hbm, wv_hbm, wo_hbm,
    pooled_ref, attended_ref,
    conv_w, wq, wk, wv, wo,
    pad, taps, edge_out, edge_in, outgoing, got, q_rows, k_rows, v_rows, mixed, back,
    conv_sem, w_sem, edge_send, edge_recv, pack_sems, back_sems, twin_sems,
):
    channels = x_ref.shape[-1]
    head = channels // HEADS
    part = channels // 2
    half = rows // 2
    reach = 2 * DILATE
    slots = 2 * seqs
    idle = (GROUP - slots) // 2
    pitch = rows + 2 * reach
    me = lax.axis_index("seq")
    mine = lax.rem(me, GROUP)
    block = me - mine
    slot = mine - idle
    active = jnp.logical_and(slot >= 0, slot < slots)

    tiles = channels // COLUMN_TILE
    conv_copies = []
    for j in range(tiles):
        cols = pl.ds(j * COLUMN_TILE, COLUMN_TILE)
        conv_copies.append(
            pltpu.make_async_copy(conv_hbm.at[:, cols], conv_w.at[:, cols], conv_sem.at[j])
        )
    w_copies = [
        pltpu.make_async_copy(a, b, w_sem.at[i])
        for i, (a, b) in enumerate(((wq_hbm, wq), (wk_hbm, wk), (wv_hbm, wv), (wo_hbm, wo)))
    ]
    barrier = pltpu.get_barrier_semaphore()

    def greet(k, carry):
        pl.semaphore_signal(
            barrier, inc=1, device_id={"seq": lax.rem(me + k, n)}, device_id_type=MESH
        )
        return carry

    lax.fori_loop(1, n, greet, 0)
    for copy in conv_copies + w_copies:
        copy.start()

    for b in range(seqs):
        edge_out[0, b * reach : (b + 1) * reach, :] = x_ref[b, :8, :].astype(jnp.float32)[:reach]
        edge_out[1, b * reach : (b + 1) * reach, :] = x_ref[b, rows - 8 :, :].astype(jnp.float32)[
            8 - reach :
        ]
    pl.semaphore_wait(barrier, n - 1)

    def edge(side, target):
        return pltpu.make_async_remote_copy(
            src_ref=edge_out.at[side],
            dst_ref=edge_in.at[side],
            send_sem=edge_send.at[side],
            recv_sem=edge_recv.at[side],
            device_id={"seq": target},
            device_id_type=MESH,
        )

    to_left = edge(0, lax.rem(me + n - 1, n))
    to_right = edge(1, lax.rem(me + 1, n))
    to_left.start()
    to_right.start()
    strips = channels // LANES
    for b in range(seqs):
        for j in range(strips):
            strip = slice(j * LANES, (j + 1) * LANES)
            pad[j, b * pitch + reach : b * pitch + reach + rows, :] = x_ref[b, :, strip].astype(
                jnp.float32
            )
    to_left.wait()
    to_right.wait()
    has_left = jnp.where(me > 0, 1.0, 0.0).astype(jnp.float32)
    has_right = jnp.where(me < n - 1, 1.0, 0.0).astype(jnp.float32)
    for b in range(seqs):
        for j in range(strips):
            strip = slice(j * LANES, (j + 1) * LANES)
            pad[j, b * pitch : b * pitch + reach, :] = (
                edge_in[1, b * reach : (b + 1) * reach, strip] * has_left
            )
            pad[j, b * pitch + reach + rows : (b + 1) * pitch, :] = (
                edge_in[0, b * reach : (b + 1) * reach, strip] * has_right
            )

    sends = seqs * (n // GROUP)
    core = lax.rem(me, 2)
    twin = me + 1 - 2 * core
    pack_send, pack_recv, pack_local = (pack_sems.at[i] for i in range(3))
    back_send, back_recv, back_local = (back_sems.at[i] for i in range(3))
    window = jnp.clip(slot, 0, slots - 1) // 2
    lanes = pl.ds(pl.multiple_of(lax.rem(jnp.clip(slot, 0, slots - 1), 2) * part, LANES), part)
    own = pltpu.make_async_copy(outgoing.at[window], got.at[me], pack_local)

    count = seqs * half
    middle = (TAPS // 2) * channels
    stage = seqs // STAGES
    for p in range(STAGES):
        first = 2 * p * stage * half
        for t in range(TAPS):
            for parity in range(2):
                for b in range(stage):
                    start = (p * stage + b) * pitch + t * DILATE + parity
                    to = first + (parity * stage + b) * half
                    for j in range(strips):
                        at = t * channels + j * LANES
                        taps[to : to + half, at : at + LANES] = (
                            pad[j, pl.ds(start, half, stride=2), :]
                        ).astype(jnp.bfloat16)
        some = stage * half
        held = slice(first, first + 2 * some)
        mean_rows = slice(p * some, (p + 1) * some)
        squares = jnp.zeros((some, 1), jnp.float32)
        for j in range(tiles):
            if p == 0:
                conv_copies[j].wait()
            cols = slice(j * COLUMN_TILE, (j + 1) * COLUMN_TILE)
            conv_sum = jnp.dot(taps[held], conv_w[:, cols], preferred_element_type=jnp.float32)
            here = taps[held, middle + j * COLUMN_TILE : middle + (j + 1) * COLUMN_TILE]
            encoded = here.astype(jnp.float32) + jax.nn.gelu(conv_sum)
            pooled = ((encoded[:some] + encoded[some:]) * 0.5).astype(jnp.bfloat16)
            pooled_ref[mean_rows, cols] = pooled
            wide = pooled.astype(jnp.float32)
            squares = squares + jnp.sum(wide * wide, axis=-1, keepdims=True)
        shrink = lax.rsqrt(squares * (1.0 / channels) + 1e-06)
        normed = (
            pooled_ref[mean_rows, :].astype(jnp.float32) * shrink * gain_ref[...].reshape(1, channels)
        ).astype(jnp.bfloat16)
        for b in range(stage):
            outgoing[p * stage + b] = normed[b * half : (b + 1) * half]

        @pl.when(jnp.logical_and(active, window // stage == p))
        def _():
            own.start()

        def scatter(k, carry, p=p):
            to = p * stage + lax.rem(k + mine // 2, stage)
            target = (k // stage) * GROUP + idle + 2 * to + core

            @pl.when(target != me)
            def _():
                pltpu.make_async_remote_copy(
                    src_ref=outgoing.at[to],
                    dst_ref=got.at[me],
                    send_sem=pack_send,
                    recv_sem=pack_recv,
                    device_id={"seq": target},
                    device_id_type=MESH,
                ).start()

            return carry

        lax.fori_loop(0, stage * (n // GROUP), scatter, 0)
    for copy in w_copies:
        copy.wait()

    def settle(ref, count, sem):
        some = ref.at[pl.ds(0, count)]
        pltpu.make_async_copy(some, some, sem).wait()

    kept = pltpu.make_async_copy(mixed.at[mine], back.at[jnp.clip(slot, 0, slots - 1)], back_local)
    factor = math.log2(math.e) / math.sqrt(head)

    @pl.when(active)
    def _():
        own.wait()
        settle(got, n // 2 - 1, pack_recv)

        def relay(i, carry):
            pltpu.make_async_remote_copy(
                src_ref=got.at[2 * i + core],
                dst_ref=got.at[2 * i + core],
                send_sem=twin_sems.at[0],
                recv_sem=twin_sems.at[1],
                device_id={"seq": twin},
                device_id_type=MESH,
            ).start()
            return carry

        lax.fori_loop(0, n // 2, relay, 0)
        settle(got, n // 2, twin_sems.at[1])

        def project(i, carry):
            made = got[pl.ds(i * GROUP, GROUP)].reshape(GROUP * half, channels)
            at = pl.ds(pl.multiple_of(i * (GROUP * half), GROUP * half), GROUP * half)
            k_rows[at, :] = jnp.dot(
                made, wk[:, lanes], preferred_element_type=jnp.float32
            ).astype(jnp.bfloat16)
            v_rows[at, :] = jnp.dot(
                made, wv[:, lanes], preferred_element_type=jnp.float32
            ).astype(jnp.bfloat16)
            return carry

        lax.fori_loop(0, n // GROUP, project, 0)
        asking = got[pl.ds(block, GROUP)].reshape(GROUP * half, channels)
        q_rows[...] = jnp.dot(
            asking, wq[:, lanes], preferred_element_type=jnp.float32
        ).astype(jnp.bfloat16)
        sources = QUERY_ROWS // half
        for q in range(GROUP // sources):
            outs = []
            for h in range(HEADS // 2):
                of_head = slice(h * head, (h + 1) * head)
                scores = lax.dot_general(
                    q_rows[q * QUERY_ROWS : (q + 1) * QUERY_ROWS, of_head],
                    k_rows[:, of_head],
                    (((1,), (1,)), ((), ())),
                    preferred_element_type=jnp.float32,
                )
                top = jnp.max(scores, axis=-1, keepdims=True)
                terms = jnp.exp2((scores - top) * factor)
                row_sum = jnp.sum(terms, axis=-1, keepdims=True)
                out = jnp.dot(
                    terms.astype(jnp.bfloat16),
                    v_rows[:, of_head],
                    preferred_element_type=jnp.float32,
                )
                outs.append(out / row_sum)
            joined = jnp.concatenate(outs, axis=-1).astype(jnp.bfloat16)
            mixed[q * sources : (q + 1) * sources] = joined.reshape(sources, half, part)
            for k in range(q * sources, (q + 1) * sources):

                @pl.when(mine != k)
                def _(k=k):
                    pltpu.make_async_remote_copy(
                        src_ref=mixed.at[k],
                        dst_ref=back.at[slot],
                        send_sem=back_send,
                        recv_sem=back_recv,
                        device_id={"seq": block + k},
                        device_id_type=MESH,
                    ).start()

                @pl.when(mine == k)
                def _():
                    kept.start()

        kept.wait()
        settle(back, slots - 1, back_recv)
        settle(mixed, GROUP - 1, back_send)
        settle(got, n // 2, twin_sems.at[0])
        settle(got, sends - 1, pack_send)

    @pl.when(jnp.logical_not(active))
    def _():
        settle(back, slots, back_recv)
        settle(got, sends, pack_send)

    attended = jnp.zeros((count, channels), jnp.float32)
    for i in range(2):
        joined = jnp.concatenate([back[2 * b + i] for b in range(seqs)], axis=0)
        attended = attended + jnp.dot(
            joined, wo[i * part : (i + 1) * part, :], preferred_element_type=jnp.float32
        )
    attended_ref[...] = attended.astype(jnp.bfloat16)


def on_device(dna_rows, conv_weight, norm_gain, w_query, w_key, w_value, w_out):
    n = lax.axis_size("seq")
    seqs, rows, channels = dna_rows.shape
    half = rows // 2
    part = channels // 2
    reach = 2 * DILATE
    bf16, f32 = jnp.bfloat16, jnp.float32
    vmem = pl.BlockSpec(memory_space=pltpu.VMEM)
    far = pl.BlockSpec(memory_space=pl.ANY)
    square = pltpu.VMEM((channels, channels), bf16)
    dma = pltpu.SemaphoreType.DMA
    pooled, attended = pl.pallas_call(
        functools.partial(kernel, n, seqs, rows),
        out_shape=[jax.ShapeDtypeStruct((seqs * half, channels), bf16)] * 2,
        in_specs=[vmem, far, vmem, far, far, far, far],
        out_specs=[vmem, vmem],
        scratch_shapes=[
            pltpu.VMEM((TAPS * channels, channels), bf16),
            square, square, square, square,
            pltpu.VMEM((channels // LANES, seqs * (rows + 2 * reach), LANES), f32),
            pltpu.VMEM((seqs * rows, TAPS * channels), bf16),
            pltpu.VMEM((2, seqs * reach, channels), f32),
            pltpu.VMEM((2, seqs * reach, channels), f32),
            pltpu.VMEM((seqs, half, channels), bf16),
            pltpu.VMEM((n, half, channels), bf16),
            pltpu.VMEM((GROUP * half, part), bf16),
            pltpu.VMEM((n * half, part), bf16),
            pltpu.VMEM((n * half, part), bf16),
            pltpu.VMEM((GROUP, half, part), bf16),
            pltpu.VMEM((2 * seqs, half, part), bf16),
            dma((channels // COLUMN_TILE,)), dma((4,)),
            dma((2,)), dma((2,)),
            dma((3,)), dma((3,)), dma((2,)),
        ],
        compiler_params=pltpu.CompilerParams(
            collective_id=0, has_side_effects=True, vmem_limit_bytes=56 * 1024 * 1024
        ),
    )(
        dna_rows,
        conv_weight.reshape(TAPS * channels, channels),
        norm_gain,
        w_query, w_key, w_value, w_out,
    )
    return pooled.reshape(seqs, half, channels), attended.reshape(seqs, half, channels)


def solution(mesh):
    placed = (P("groups", "seq", None), P(), P(), P(), P(), P(), P())
    return jax.shard_map(
        on_device,
        mesh=mesh,
        in_specs=placed,
        out_specs=(P("groups", "seq", None), P("groups", "seq", None)),
        check_vma=False,
    )
```
